1024 devices in a mesh: pipe: 2 (over x_lo), row: 32 (over z, core), col: 16 (over y, x_hi).
Axes of the slice: x: 4 (x_hi: 2, x_lo: 2; x = x_hi * 2 + x_lo), y: 8, z: 16, core: 2. Of those that a mesh axis runs over, the one named last changes fastest.
Arguments:
- grad_output: bfloat16 [4096, 4096], P('row', 'col'), may hold values from -6 to 6
- queries: bfloat16 [2, 4096, 4096], P('pipe', 'row', 'col'), may hold values from -70 to 70
- keys: bfloat16 [2, 4096, 4096], P('pipe', 'row', 'col'), may hold values from -8 to 8
- values: bfloat16 [2, 4096, 4096], P('pipe', 'row', 'col'), may hold values from -6 to 6
- value_weight: bfloat16 [2, 4096, 4096], P('pipe', 'col', 'row'), may hold values from -0.375 to 0.375
- random_table: int32 [2, 64, 32, 3], P('pipe', None, 'col'), may hold values from 0 to 63, as said below
Outputs:
- input_grads: bfloat16 [2, 4096, 4096], P('pipe', 'row', 'col')
- query_grads: bfloat16 [2, 4096, 4096], P('pipe', 'row', 'col')
- key_grads: bfloat16 [2, 4096, 4096], P('pipe', 'row', 'col')
The draws below stay inside these ranges and needn't reach their ends.
Inputs may be any that keep to these rules, and one draw needn't show every extreme that they name: `random_table`: for each section, the random blocks that one aligned group of 2 query blocks names for one aligned group of 2 heads fall at most 1 times into any one aligned group of 2 key blocks, and exactly 1 times into some group.
All inputs are finite; a program needn't handle non-finite values.
Results may differ from the reference program's by a relative error of at most 0.03.
Values may be sent and summed in bfloat16 or wider, within the bound.
A program may use at most 32 MiB of HBM per device.

```python
import math
import jax
import jax.numpy as jnp
from jax import lax

HEADS = 32
HEAD_DIM = 128
WIDTH = 4096
BLOCK = 64
RANDOMS = 3
SECTIONS = 2
SEQUENCE = 4096
BLOCKS = 64
QBLOCKS_DEV = 2
HEADS_DEV = 2
SLOTS = 1


def draw_pair(key):
    base = jax.random.fold_in(key, 7)
    key_query, key_key = jax.random.split(base, 2)
    shape = (SECTIONS, SEQUENCE, HEADS, HEAD_DIM)
    queries = jax.random.normal(key_query, shape, jnp.float32)
    keys = jax.random.normal(key_key, shape, jnp.float32)
    return (queries.reshape(SECTIONS, SEQUENCE, WIDTH), keys.reshape(SECTIONS, SEQUENCE, WIDTH))


def draw_queries(key, part):
    return draw_pair(key)[0].astype(jnp.bfloat16)


def draw_keys(key, part):
    return draw_pair(key)[1].astype(jnp.bfloat16)


def draw_random_table(key, part):
    base = jax.random.fold_in(key, 23)
    row_groups = BLOCKS // QBLOCKS_DEV
    head_groups = HEADS // HEADS_DEV
    per_group = QBLOCKS_DEV * HEADS_DEV * RANDOMS
    group_keys = jax.random.split(base, SECTIONS * row_groups * head_groups)

    def one_group(group_key):
        key_order, key_local = jax.random.split(group_key)
        order = jax.random.permutation(key_order, row_groups * SLOTS)[:per_group]
        source = order // SLOTS
        local = jax.random.randint(key_local, (per_group,), 0, QBLOCKS_DEV)
        return (source * QBLOCKS_DEV + local).astype(jnp.int32)
    table = jax.vmap(one_group)(group_keys)
    table = table.reshape(SECTIONS, row_groups, head_groups, QBLOCKS_DEV, HEADS_DEV, RANDOMS)
    table = table.transpose(0, 1, 3, 2, 4, 5)
    return table.reshape(SECTIONS, BLOCKS, HEADS, RANDOMS)


def raised(entries, rng, source, target, parts, factor):
    owner, partner = [(jnp.arange(entries.shape[axis_at]) // (entries.shape[axis_at] // parts)).reshape([-1 if axis == axis_at else 1 for axis in range(entries.ndim)]) for axis_at in (source, target)]
    chosen = jax.random.permutation(rng, parts)[partner]
    strong = (owner == chosen) | (owner == (partner + parts // 2) % parts)
    return jnp.where(strong, factor * entries, entries)


def shard_levels(key, extent, shards, least, high):
    def one(dim, blocks):
        heights = jax.random.uniform(jax.random.fold_in(jax.random.fold_in(key, 6), dim), (blocks,), jnp.float32, least / len(shards), high / len(shards))
        return jnp.repeat(jnp.exp(heights), extent[dim] // blocks).reshape((-1,) + (1,) * (len(extent) - dim - 1))

    factor_of = one(*shards[0])
    for cut in shards[1:]:
        factor_of = factor_of * one(*cut)
    return factor_of


def gaussian(rng, dims, spread, most, pieces=(), kind=jnp.bfloat16):
    factor_of = shard_levels(rng, dims, pieces, -0.22, 0.18) if pieces else 1.0
    values = jax.random.normal(rng, dims, jnp.float32) * spread * factor_of
    return jnp.minimum(jnp.maximum(values, -most), most).astype(kind)


def gaussian_with(key, extent, spread, most, cuts, heavy, kind=jnp.bfloat16):
    entries = spread * jax.random.normal(key, extent, jnp.float32)
    if cuts:
        entries = entries * shard_levels(key, extent, cuts, -0.22, 0.18)
    return jnp.clip(raised(entries, jax.random.fold_in(key, 3), *heavy), -most, most).astype(kind)


def setup_inputs(seed: int = 0) -> dict:
    splits = jax.random.split(jax.random.key(seed), 7)
    grad_output = gaussian(splits[0], (SEQUENCE, WIDTH), 1.0, 6.0, ((0, 32), (1, 16)))
    queries = draw_queries(jax.random.fold_in(splits[6], 71), 0)
    keys = draw_keys(jax.random.fold_in(splits[6], 71), 0)
    values = gaussian(splits[3], (SECTIONS, SEQUENCE, WIDTH), 1.0, 6.0, ((0, 2), (1, 32), (2, 16)))
    value_weight = gaussian_with(splits[4], (SECTIONS, WIDTH, WIDTH), (WIDTH // 4) ** -0.5, 0.375, ((0, 2), (1, 16), (2, 32)), (2, 1, 32, 2.75))
    random_table = draw_random_table(jax.random.fold_in(splits[6], 71), 0)
    return {"grad_output": grad_output, "queries": queries, "keys": keys, "values": values, "value_weight": value_weight, "random_table": random_table}


def rounded(array):
    return lax.optimization_barrier(array.astype(jnp.bfloat16)).astype(jnp.float32)

def section_backward(upstream, queries, keys, values, weight, table):
    scale = 1.0 / math.sqrt(HEAD_DIM)
    block_ids = jnp.arange(BLOCKS, dtype=jnp.int32)
    window = jnp.stack([block_ids - 1, block_ids, block_ids + 1], axis=1)
    window_ok = (window >= 0) & (window < BLOCKS)

    def one_head(head):

        def pick(array):
            part = lax.dynamic_slice_in_dim(array, head * HEAD_DIM, HEAD_DIM, 1)
            return part.astype(jnp.float32).reshape(BLOCKS, BLOCK, HEAD_DIM)
        query = pick(queries)
        key = pick(keys)
        value = pick(values)
        grad = pick(upstream)
        chosen = lax.dynamic_index_in_dim(table, head, 1, keepdims=False).astype(jnp.int32)
        tiles = jnp.concatenate([jnp.clip(window, 0, BLOCKS - 1), chosen], axis=1).astype(jnp.int32)
        valid = jnp.concatenate([window_ok, jnp.ones((BLOCKS, RANDOMS), bool)], axis=1)
        key_tiles = key[tiles]
        value_tiles = value[tiles]
        scores = jnp.einsum('nid,ntjd->nitj', query, key_tiles) * scale
        scores = jnp.where(valid[:, None, :, None], scores, -1e+30)
        top = lax.optimization_barrier(jnp.max(scores, axis=(2, 3), keepdims=True))
        log_total = top + jnp.log(lax.optimization_barrier(jnp.sum(jnp.exp(scores - top), axis=(2, 3), keepdims=True)))
        probs = jnp.exp(scores - log_total)
        probs_low = rounded(probs)
        outputs = jnp.einsum('nitj,ntjd->nid', probs_low, value_tiles)
        delta = lax.optimization_barrier(jnp.sum(grad * outputs, axis=2))[:, :, None, None]
        dprobs = jnp.einsum('nid,ntjd->nitj', grad, value_tiles)
        dscores = rounded(probs * (dprobs - delta) * scale)
        query_grad = jnp.einsum('nitj,ntjd->nid', dscores, key_tiles)
        key_terms = rounded(jnp.einsum('nitj,nid->ntjd', dscores, query))
        value_terms = rounded(jnp.einsum('nitj,nid->ntjd', probs_low, grad))
        flat = tiles.reshape(-1)
        key_grad = jax.ops.segment_sum(key_terms.reshape(-1, BLOCK, HEAD_DIM), flat, BLOCKS)
        value_grad = jax.ops.segment_sum(value_terms.reshape(-1, BLOCK, HEAD_DIM), flat, BLOCKS)
        return (query_grad.astype(jnp.bfloat16).reshape(SEQUENCE, HEAD_DIM), key_grad.astype(jnp.bfloat16).reshape(SEQUENCE, HEAD_DIM), value_grad.astype(jnp.bfloat16).reshape(SEQUENCE, HEAD_DIM))
    per_head = lax.map(one_head, jnp.arange(HEADS, dtype=jnp.int32))

    def merge_heads(array):
        return array.transpose(1, 0, 2).reshape(SEQUENCE, WIDTH)
    query_grads = merge_heads(per_head[0])
    key_grads = merge_heads(per_head[1])
    value_grads = merge_heads(per_head[2])
    projected = jnp.dot(value_grads, weight.T, preferred_element_type=jnp.float32)
    input_grads = (upstream.astype(jnp.float32) + projected).astype(jnp.bfloat16)
    return (input_grads, query_grads, key_grads)

def reference(grad_output, queries, keys, values, value_weight, random_table):
    upstream = grad_output
    input_list = [None] * SECTIONS
    query_list = [None] * SECTIONS
    key_list = [None] * SECTIONS
    for section in reversed(range(SECTIONS)):
        results = section_backward(upstream, queries[section], keys[section], values[section], value_weight[section], random_table[section])
        input_list[section] = results[0]
        query_list[section] = results[1]
        key_list[section] = results[2]
        upstream = results[0]
    return (jnp.stack(input_list), jnp.stack(query_list), jnp.stack(key_list))
```

```python
import math

import jax
import jax.numpy as jnp
from jax import lax
from jax.experimental import pallas as pl
from jax.experimental.pallas import tpu as pltpu
from jax.sharding import PartitionSpec as P

HEAD_DIM = 128
BLOCK = 64
RANDOMS = 3
HEADS_DEV = 2
QBLOCKS = 2
TILES = 3 + RANDOMS
ENTRIES = QBLOCKS * RANDOMS
ZERO, RIM_LEFT, RIM_RIGHT, SLOTS = ENTRIES, ENTRIES + 1, ENTRIES + 2, ENTRIES + 3
MESH = pl.DeviceIdType.MESH
BF16 = jnp.bfloat16
F32 = jnp.float32


def drive(*streams):
    streams = list(streams)
    while streams:
        for stream in list(streams):
            if next(stream, "end") == "end":
                streams.remove(stream)


def lanes(head):
    return pl.ds(head * HEAD_DIM, HEAD_DIM)


def kernel(
    rows,
    cols,
    table,
    grad,
    query,
    key,
    value,
    weight,
    input_out,
    query_out,
    key_out,
    key_all,
    value_all,
    weight_all,
    grad_all,
    up,
    probs,
    acc,
    v_own,
    v_sib,
    v_local,
    v_send,
    v_recv,
    k_own,
    k_sib,
    k_local,
    k_send,
    k_recv,
    ring_send,
    ring_recv,
    sib_send,
    sib_recv,
    col_send,
    col_recv,
    sum_send,
    sum_recv,
    one_send,
    one_recv,
):
    chips = rows // 2
    ycount = cols // 2
    scale = 1.0 / math.sqrt(HEAD_DIM)
    pipe = lax.axis_index("pipe")
    row = lax.axis_index("row")
    col = lax.axis_index("col")
    chip, core = row // 2, lax.rem(row, 2)
    ypos, xpos = col // 2, lax.rem(col, 2)
    sibling = row + 1 - 2 * core
    row_next = ({"row": lax.rem(row + 2, rows)}, {"row": lax.rem(row + rows - 2, rows)})
    col_next = ({"col": lax.rem(col + 2, cols)}, {"col": lax.rem(col + cols - 2, cols)})
    to_sibling = {"row": sibling}
    to_partner = {"col": col + 1 - 2 * xpos}
    to_pipe = {"pipe": 1 - pipe}

    barrier = pltpu.get_barrier_semaphore()
    for device in (*row_next, *col_next, to_sibling, to_partner, to_pipe):
        pl.semaphore_signal(barrier, inc=1, device_id=device, device_id_type=MESH)
    pl.semaphore_wait(barrier, 7)

    def remote(src, dst, send, recv, device):
        return pltpu.make_async_remote_copy(
            src_ref=src,
            dst_ref=dst,
            send_sem=send,
            recv_sem=recv,
            device_id=device,
            device_id_type=MESH,
        )

    def gather(sent, buf, pos, size, entry, devices, send, recv, shared=None, second=None, arrive=None):
        half = size // 2

        def ref(offset, item):
            return buf.at[entry(lax.rem(pos + offset + size, size), item)]

        def copy(way, step, item):
            offset = step if way else -step
            return remote(
                ref(offset, item),
                ref(offset, item),
                send.at[way, step, item],
                recv.at[way, step, item],
                devices[way],
            )

        def push(way, step, item):
            if step < half - 1 or (step == half - 1 and way == item):
                made = copy(way, step, item)
                made.start()
                sent.append(made)

        def arrived(way, step, item):
            offset = step if way else -step
            remote(
                ref(offset, item),
                ref(offset, item),
                send.at[way, step - 1, item],
                recv.at[way, step - 1, item],
                devices[way],
            ).wait_recv()

        def share(offset):
            if shared is not None:
                shared(offset)

        for item in range(2):
            if item == 1 and second is not None:
                second()
            for way in range(2):
                push(way, 0, item)
        share(0)
        if arrive is not None:
            arrive(0, 0)
            arrive(0, 1)
        yield
        for step in range(1, half):
            for item in range(2):
                for way in range(2):
                    arrived(way, step, item)
                    push(way, step, item)
                if item == 1:
                    share(-step)
                    share(step)
                if arrive is not None:
                    arrive(-step, item)
                    arrive(step, item)
                yield
        for way in range(2):
            arrived(way, half, way)
        share(half)
        if arrive is not None:
            arrive(half, 0)
            arrive(half, 1)
        yield

    def row_gather(sent, which, buf):
        shares = []

        def entry(place, item):
            return 4 * place + 2 * core + item

        def shared(offset):
            place = lax.rem(chip + offset + chips, chips)
            block = buf.at[pl.ds(4 * place + 2 * core, 2)]
            slot = (offset + chips) % chips
            made = remote(
                block, block, sib_send.at[which, slot], sib_recv.at[which, slot], to_sibling
            )
            made.start()
            shares.append(made)

        yield from gather(
            sent,
            buf,
            chip,
            chips,
            entry,
            row_next,
            ring_send.at[which],
            ring_recv.at[which],
            shared=shared,
        )
        for made in shares:
            made.wait_recv()
        sent.extend(shares)

    def tile_ids(n, head):
        block = 2 * row + n
        ids = [
            lax.rem(block + 2 * rows - 1, 2 * rows),
            block,
            lax.rem(block + 1, 2 * rows),
        ]
        for t in range(RANDOMS):
            ids.append(table[row * 12 + n * 6 + head * 3 + t])
        return ids

    def tiles(buf, n, head):
        return jnp.concatenate([buf[i, :, lanes(head)] for i in tile_ids(n, head)], axis=0)

    def rows_of(ref, n, head):
        return ref[pl.ds(n * BLOCK, BLOCK), lanes(head)]

    def make_probs():
        for n in range(QBLOCKS):
            for head in range(HEADS_DEV):
                scores = scale * lax.dot_general(
                    rows_of(query, n, head),
                    tiles(key_all, n, head),
                    (((1,), (1,)), ((), ())),
                    preferred_element_type=F32,
                )
                place = lax.broadcasted_iota(jnp.int32, scores.shape, 1) // BLOCK
                block = 2 * row + n
                gone = jnp.where(block == 0, 0, -1)
                gone_right = jnp.where(block == 2 * rows - 1, 2, -1)
                scores = jnp.where((place == gone) | (place == gone_right), -1e30, scores)
                top = jnp.max(scores, axis=1, keepdims=True)
                total = jnp.sum(jnp.exp(scores - top), axis=1, keepdims=True)
                probs[n, head] = jnp.exp(scores - (top + jnp.log(total)))

    def keep_terms(n, head, terms, own, local):
        terms = terms.astype(BF16)
        part = [terms[t * BLOCK : (t + 1) * BLOCK] for t in range(TILES)]
        for t in range(RANDOMS):
            own[head * SLOTS + n * RANDOMS + t] = part[3 + t]
        if n == 0:
            own[head * SLOTS + ZERO] = jnp.zeros_like(part[0])
            own[head * SLOTS + RIM_LEFT] = part[0]
            local[0, :, lanes(head)] = part[1].astype(F32)
            local[1, :, lanes(head)] = part[2].astype(F32)
        else:
            local[0, :, lanes(head)] += part[0].astype(F32)
            local[1, :, lanes(head)] += part[1].astype(F32)
            own[head * SLOTS + RIM_RIGHT] = part[2]

    def transposed_dot(left, right):
        return lax.dot_general(left, right, (((0,), (0,)), ((), ())), preferred_element_type=F32)

    def value_terms():
        for n in range(QBLOCKS):
            for head in range(HEADS_DEV):
                low = probs[n, head].astype(BF16)
                keep_terms(n, head, transposed_dot(low, rows_of(up, n, head)), v_own, v_local)

    def key_terms():
        for n in range(QBLOCKS):
            for head in range(HEADS_DEV):
                prob = probs[n, head]
                dprobs = lax.dot_general(
                    rows_of(up, n, head),
                    tiles(value_all, n, head),
                    (((1,), (1,)), ((), ())),
                    preferred_element_type=F32,
                )
                low = prob.astype(BF16).astype(F32)
                delta = jnp.sum(low * dprobs, axis=1, keepdims=True)
                dscores = (prob * (dprobs - delta) * scale).astype(BF16)
                query_out[pl.ds(n * BLOCK, BLOCK), lanes(head)] = jnp.dot(
                    dscores, tiles(key_all, n, head), preferred_element_type=F32
                ).astype(BF16)
                keep_terms(
                    n, head, transposed_dot(dscores, rows_of(query, n, head)), k_own, k_local
                )
                yield

    def find(owner, block, head):
        found = ZERO
        for n in range(QBLOCKS):
            for t in range(RANDOMS):
                named = table[owner * 12 + n * 6 + head * 3 + t]
                found = jnp.where(named == block, n * RANDOMS + t, found)
        return found

    def reduce(sent, which, own, sib, local, sbuf, rbuf, result):
        half = chips // 2

        def contribution(offset, part, head):
            place = lax.rem(chip + offset + chips, chips)
            block = 4 * place + 2 * core + part
            found = own[head * SLOTS + find(row, block, head)].astype(F32)
            found += sib[head * SLOTS + find(sibling, block, head)].astype(F32)
            rim = None
            if (offset, part) == (0, 0):
                rim = jnp.where(core == 1, RIM_RIGHT, ZERO)
            if (offset, part) == (0, 1):
                rim = jnp.where(core == 0, RIM_LEFT, ZERO)
            if (offset, part) == (1, 0):
                rim = jnp.where(core == 0, RIM_RIGHT, ZERO)
            if (offset, part) == (-1, 1):
                rim = jnp.where(core == 1, RIM_LEFT, ZERO)
            if rim is not None:
                found += sib[head * SLOTS + rim].astype(F32)
            return found

        def copy(way, step, part):
            return remote(
                sbuf.at[way, step, part],
                rbuf.at[way, step, part],
                sum_send.at[which, way, step, part],
                sum_recv.at[which, way, step, part],
                row_next[way],
            )

        exchange = remote(own, sib, one_send.at[which], one_recv.at[which], to_sibling)
        exchange.start()
        exchange.wait_recv()
        sent.append(exchange)
        for step in range(half):
            for part in range(2):
                for way in range(2):
                    if step == 0 and part != way:
                        continue
                    distance = half - step
                    offset = -distance if way else distance
                    terms = [contribution(offset, part, head) for head in range(HEADS_DEV)]
                    if step > 1 or (step == 1 and part == way):
                        copy(way, step - 1, part).wait_recv()
                        for head in range(HEADS_DEV):
                            terms[head] += rbuf[way, step - 1, part, :, lanes(head)].astype(F32)
                    for head in range(HEADS_DEV):
                        sbuf[way, step, part, :, lanes(head)] = terms[head].astype(BF16)
                    made = copy(way, step, part)
                    made.start()
                    sent.append(made)
                yield
        for part in range(2):
            total = local[part] + jnp.concatenate(
                [contribution(0, part, head) for head in range(HEADS_DEV)], axis=1
            )
            for way in range(2):
                copy(way, half - 1, part).wait_recv()
                total += rbuf[way, half - 1, part].astype(F32)
            result(part, total.astype(BF16))
        yield

    def keep_value_grad(part, total):
        grad_all[col, pl.ds(part * BLOCK, BLOCK)] = total

    def keep_key_grad(part, total):
        key_out[pl.ds(part * BLOCK, BLOCK)] = total

    def col_entry(place, item):
        own = 2 * place + xpos
        return own if item == 0 else 2 * place + 1 - xpos

    def project(place):
        total = acc[...]
        for part in range(2):
            total += lax.dot_general(
                grad_all[place, :, lanes(part)],
                weight_all[pl.ds(4 * place + 2 * part, 2)].reshape(2 * HEAD_DIM, HEAD_DIM),
                (((1,), (1,)), ((), ())),
                preferred_element_type=F32,
            )
        acc[...] = total

    def col_gather(sent, arrive):
        def exchange():
            return remote(
                grad_all.at[col], grad_all.at[col], one_send.at[2], one_recv.at[2], to_partner
            )

        made = exchange()
        made.start()
        sent.append(made)

        def on_arrive(offset, item):
            if arrive:
                project(col_entry(lax.rem(ypos + offset + ycount, ycount), item))

        yield from gather(
            sent,
            grad_all,
            ypos,
            ycount,
            col_entry,
            col_next,
            col_send,
            col_recv,
            second=lambda: exchange().wait_recv(),
            arrive=on_arrive,
        )

    def upstream_copy():
        return remote(input_out, up, one_send.at[3], one_recv.at[3], to_pipe)

    def key_reduce(sent):
        yield from reduce(sent, 1, k_own, k_sib, k_local, k_send, k_recv, keep_key_grad)

    def value_reduce(sent):
        yield from reduce(sent, 0, v_own, v_sib, v_local, v_send, v_recv, keep_value_grad)

    own_rows = pl.ds(2 * row, 2)
    key_all[own_rows] = key[...].reshape(2, BLOCK, key.shape[1])
    value_all[own_rows] = value[...].reshape(2, BLOCK, value.shape[1])
    weight_all[own_rows] = weight[...].reshape(2, HEAD_DIM, HEAD_DIM)

    @pl.when(pipe == 1)
    def _():
        sent = []
        drive(row_gather(sent, 0, key_all))
        make_probs()
        up[...] = grad[...]
        value_terms()
        drive(value_reduce(sent))
        acc[...] = up[...].astype(F32)
        drive(col_gather(sent, False), row_gather(sent, 1, weight_all))

        def step(place, carry):
            project(place)
            return carry

        lax.fori_loop(0, cols, step, 0)
        input_out[...] = acc[...].astype(BF16)
        made = upstream_copy()
        made.start()
        drive(row_gather(sent, 2, value_all))
        drive(key_terms())
        drive(key_reduce(sent))
        made.wait_send()
        for made in sent:
            made.wait_send()

    @pl.when(pipe == 0)
    def _():
        sent = []
        drive(row_gather(sent, 0, key_all))
        make_probs()
        drive(row_gather(sent, 1, weight_all))
        drive(row_gather(sent, 2, value_all))
        upstream_copy().wait_recv()
        value_terms()
        drive(value_reduce(sent), key_terms())
        acc[...] = up[...].astype(F32)
        drive(col_gather(sent, True), key_reduce(sent))
        input_out[...] = acc[...].astype(BF16)
        for made in sent:
            made.wait_send()


def body(grad_output, queries, keys, values, value_weight, random_table):
    rows = lax.axis_size("row")
    cols = lax.axis_size("col")
    tokens, features = grad_output.shape
    chips, ycount = rows // 2, cols // 2
    vmem = pl.BlockSpec(memory_space=pltpu.VMEM)
    dma = pltpu.SemaphoreType.DMA
    out = jax.ShapeDtypeStruct((tokens, features), BF16)
    ring = (2, chips // 2, 2, BLOCK, features)
    terms = (HEADS_DEV * SLOTS, BLOCK, HEAD_DIM)
    reducing = [
        pltpu.VMEM(terms, BF16),
        pltpu.VMEM(terms, BF16),
        pltpu.VMEM((2, BLOCK, features), F32),
        pltpu.VMEM(ring, BF16),
        pltpu.VMEM(ring, BF16),
    ]

    def run(*refs):
        kernel(rows, cols, *refs)

    flops = 10 * 2 * tokens * features * TILES * BLOCK + 2 * tokens * features * cols * features
    grads = pl.pallas_call(
        run,
        out_shape=(out, out, out),
        in_specs=[pl.BlockSpec(memory_space=pltpu.SMEM)] + [vmem] * 5,
        out_specs=(vmem, vmem, vmem),
        scratch_shapes=[
            pltpu.VMEM((2 * rows, BLOCK, features), BF16),
            pltpu.VMEM((2 * rows, BLOCK, features), BF16),
            pltpu.VMEM((2 * rows, HEAD_DIM, HEAD_DIM), BF16),
            pltpu.VMEM((cols, tokens, features), BF16),
            pltpu.VMEM((tokens, features), BF16),
            pltpu.VMEM((QBLOCKS, HEADS_DEV, BLOCK, TILES * BLOCK), F32),
            pltpu.VMEM((tokens, features), F32),
            *reducing,
            *reducing,
            dma((3, 2, chips // 2, 2)),
            dma((3, 2, chips // 2, 2)),
            dma((3, chips)),
            dma((3, chips)),
            dma((2, ycount // 2, 2)),
            dma((2, ycount // 2, 2)),
            dma((2, 2, chips // 2, 2)),
            dma((2, 2, chips // 2, 2)),
            dma((4,)),
            dma((4,)),
        ],
        compiler_params=pltpu.CompilerParams(
            collective_id=0, has_side_effects=True, vmem_limit_bytes=40 * 2**20
        ),
        cost_estimate=pl.CostEstimate(
            flops=flops, bytes_accessed=16 * tokens * features, transcendentals=0
        ),
        name="relay",
    )(
        random_table.reshape(-1),
        grad_output,
        queries[0],
        keys[0],
        values[0],
        value_weight[0],
    )
    return tuple(array[None] for array in grads)


def solution(mesh):
    in_specs = (
        P("row", "col"),
        P("pipe", "row", "col"),
        P("pipe", "row", "col"),
        P("pipe", "row", "col"),
        P("pipe", "col", "row"),
        P("pipe", None, "col", None),
    )
    out_specs = (P("pipe", "row", "col"), P("pipe", "row", "col"), P("pipe", "row", "col"))
    return jax.shard_map(body, mesh=mesh, in_specs=in_specs, out_specs=out_specs, check_vma=False)
```

```python
import math

import jax
import jax.numpy as jnp
from jax import lax
from jax.experimental import pallas as pl
from jax.experimental.pallas import tpu as pltpu
from jax.sharding import PartitionSpec as P

HEAD_DIM = 128
BLOCK = 64
RANDOMS = 3
HEADS_DEV = 2
QBLOCKS = 2
TILES = 3 + RANDOMS
ENTRIES = QBLOCKS * RANDOMS
ZERO, RIM_LEFT, RIM_RIGHT, SLOTS = ENTRIES, ENTRIES + 1, ENTRIES + 2, ENTRIES + 3
MESH = pl.DeviceIdType.MESH
BF16 = jnp.bfloat16
F32 = jnp.float32


def drive(*streams):
    streams = list(streams)
    while streams:
        for stream in list(streams):
            if next(stream, "end") == "end":
                streams.remove(stream)


def take(stream, delay, count):
    for _ in range(delay):
        yield
    for _ in range(count):
        if next(stream, "end") == "end":
            return
        yield


def tree(half, skip):
    if not skip:
        return [(i, i + 1) for i in range(half)]
    edges = []
    for i in range(0, half, 2):
        edges += [(i, j) for j in (i + 2, i + 1) if j <= half]
    return edges


def lanes(head):
    return pl.ds(head * HEAD_DIM, HEAD_DIM)


def kernel(
    rows,
    cols,
    table,
    grad,
    query_hbm,
    key,
    value,
    weight,
    input_out,
    query_out,
    key_out,
    key_all,
    value_all,
    weight_all,
    grad_all,
    query,
    up,
    probs,
    acc,
    v_own,
    v_sib,
    v_local,
    v_send,
    v_recv,
    k_own,
    k_sib,
    k_local,
    k_send,
    k_recv,
    ring_send,
    ring_recv,
    sib_send,
    sib_recv,
    col_send,
    col_recv,
    sum_send,
    sum_recv,
    one_send,
    one_recv,
    load_sem,
):
    chips = rows // 2
    ycount = cols // 2
    scale = 1.0 / math.sqrt(HEAD_DIM)
    pipe = lax.axis_index("pipe")
    row = lax.axis_index("row")
    col = lax.axis_index("col")
    chip, core = row // 2, lax.rem(row, 2)
    ypos, xpos = col // 2, lax.rem(col, 2)
    sibling = row + 1 - 2 * core

    def chip_at(hops):
        return {"row": lax.rem(row + 2 * hops + rows, rows)}

    def place_at(hops):
        return {"col": lax.rem(col + 2 * hops + cols, cols)}

    to_sibling = {"row": sibling}
    to_partner = {"col": col + 1 - 2 * xpos}
    to_pipe = {"pipe": 1 - pipe}

    own_key = [
        pltpu.make_async_copy(key.at[i], key_all.at[2 * row + i], load_sem.at[i]) for i in range(2)
    ]
    loads = [
        pltpu.make_async_copy(weight.at[i], weight_all.at[2 * row + i], load_sem.at[2 + i])
        for i in range(2)
    ]
    loads += [
        pltpu.make_async_copy(value.at[i], value_all.at[2 * row + i], load_sem.at[4 + i])
        for i in range(2)
    ]
    loads.append(pltpu.make_async_copy(query_hbm, query, load_sem.at[6]))
    own_grad = pltpu.make_async_copy(grad, up, load_sem.at[7])
    for load in own_key + loads:
        load.start()

    barrier = pltpu.get_barrier_semaphore()
    greeted = [chip_at(hops) for hops in (1, -1, 2, -2)]
    greeted += [place_at(1), place_at(-1), to_sibling, to_partner, to_pipe]
    for device in greeted:
        pl.semaphore_signal(barrier, inc=1, device_id=device, device_id_type=MESH)
    for load in own_key:
        load.wait()
    pl.semaphore_wait(barrier, len(greeted))

    def remote(src, dst, send, recv, device):
        return pltpu.make_async_remote_copy(
            src_ref=src,
            dst_ref=dst,
            send_sem=send,
            recv_sem=recv,
            device_id=device,
            device_id_type=MESH,
        )

    def gather(sent, buf, pos, size, entry, device_at, skip, send, recv, shared=None, second=None, arrive=None):
        half = size // 2
        edges = tree(half, skip)

        def ref(offset, item):
            return buf.at[entry(lax.rem(pos + offset + size, size), item)]

        def copy(way, start, end, item, offset):
            block = ref(offset, item)
            return remote(
                block,
                block,
                send.at[way, end - 1, item],
                recv.at[way, end - 1, item],
                device_at(start - end if way else end - start),
            )

        def push(way, distance, item):
            for start, end in edges:
                if start == distance and (end < half or way == item):
                    made = copy(way, start, end, item, distance if way else -distance)
                    made.start()
                    sent.append(made)

        for item in range(2):
            if item == 1 and second is not None:
                second()
            for way in range(2):
                push(way, 0, item)
        if shared is not None:
            shared(0)
        if arrive is not None:
            arrive(0, 0)
            arrive(0, 1)
        yield
        for start, end in edges:
            for item in range(2):
                ways = [way for way in range(2) if end < half or way == item]
                for way in ways:
                    copy(way, start, end, item, end if way else -end).wait_recv()
                    push(way, end, item)
                if shared is not None and item == 1:
                    for offset in (-end, end)[: 2 if end < half else 1]:
                        shared(offset)
                if arrive is not None:
                    for way in ways:
                        arrive(end if way else -end, item)
                yield

    def row_gather(sent, which, buf, skip=True):
        shares = []

        def entry(place, item):
            return 4 * place + 2 * core + item

        def shared(offset):
            place = lax.rem(chip + offset + chips, chips)
            block = buf.at[pl.ds(4 * place + 2 * core, 2)]
            slot = (offset + chips) % chips
            made = remote(
                block, block, sib_send.at[which, slot], sib_recv.at[which, slot], to_sibling
            )
            made.start()
            shares.append(made)

        yield from gather(
            sent,
            buf,
            chip,
            chips,
            entry,
            chip_at,
            skip,
            ring_send.at[which],
            ring_recv.at[which],
            shared=shared,
        )
        for made in shares:
            made.wait_recv()
        sent.extend(shares)

    def tile_ids(n, head):
        block = 2 * row + n
        ids = [
            lax.rem(block + 2 * rows - 1, 2 * rows),
            block,
            lax.rem(block + 1, 2 * rows),
        ]
        for t in range(RANDOMS):
            ids.append(table[row * 12 + n * 6 + head * 3 + t])
        return ids

    def tiles(buf, n, head):
        return jnp.concatenate([buf[i, :, lanes(head)] for i in tile_ids(n, head)], axis=0)

    def rows_of(ref, n, head):
        return ref[pl.ds(n * BLOCK, BLOCK), lanes(head)]

    def make_probs():
        for n in range(QBLOCKS):
            for head in range(HEADS_DEV):
                scores = scale * lax.dot_general(
                    rows_of(query, n, head),
                    tiles(key_all, n, head),
                    (((1,), (1,)), ((), ())),
                    preferred_element_type=F32,
                )
                place = lax.broadcasted_iota(jnp.int32, scores.shape, 1) // BLOCK
                block = 2 * row + n
                gone = jnp.where(block == 0, 0, -1)
                gone_right = jnp.where(block == 2 * rows - 1, 2, -1)
                scores = jnp.where((place == gone) | (place == gone_right), -1e30, scores)
                top = jnp.max(scores, axis=1, keepdims=True)
                total = jnp.sum(jnp.exp(scores - top), axis=1, keepdims=True)
                probs[n, head] = jnp.exp(scores - (top + jnp.log(total)))

    def keep_terms(n, head, terms, own, local):
        terms = terms.astype(BF16)
        part = [terms[t * BLOCK : (t + 1) * BLOCK] for t in range(TILES)]
        for t in range(RANDOMS):
            own[head * SLOTS + n * RANDOMS + t] = part[3 + t]
        if n == 0:
            own[head * SLOTS + ZERO] = jnp.zeros_like(part[0])
            own[head * SLOTS + RIM_LEFT] = part[0]
            local[0, :, lanes(head)] = part[1].astype(F32)
            local[1, :, lanes(head)] = part[2].astype(F32)
        else:
            local[0, :, lanes(head)] += part[0].astype(F32)
            local[1, :, lanes(head)] += part[1].astype(F32)
            own[head * SLOTS + RIM_RIGHT] = part[2]

    def transposed_dot(left, right):
        return lax.dot_general(left, right, (((0,), (0,)), ((), ())), preferred_element_type=F32)

    def value_terms():
        for n in range(QBLOCKS):
            for head in range(HEADS_DEV):
                low = probs[n, head].astype(BF16)
                keep_terms(n, head, transposed_dot(low, rows_of(up, n, head)), v_own, v_local)

    def key_terms():
        for n in range(QBLOCKS):
            for head in range(HEADS_DEV):
                prob = probs[n, head]
                dprobs = lax.dot_general(
                    rows_of(up, n, head),
                    tiles(value_all, n, head),
                    (((1,), (1,)), ((), ())),
                    preferred_element_type=F32,
                )
                low = prob.astype(BF16).astype(F32)
                delta = jnp.sum(low * dprobs, axis=1, keepdims=True)
                dscores = (prob * (dprobs - delta) * scale).astype(BF16)
                query_out[pl.ds(n * BLOCK, BLOCK), lanes(head)] = jnp.dot(
                    dscores, tiles(key_all, n, head), preferred_element_type=F32
                ).astype(BF16)
                keep_terms(
                    n, head, transposed_dot(dscores, rows_of(query, n, head)), k_own, k_local
                )
                yield

    def find(owner, block, head):
        found = ZERO
        for n in range(QBLOCKS):
            for t in range(RANDOMS):
                named = table[owner * 12 + n * 6 + head * 3 + t]
                found = jnp.where(named == block, n * RANDOMS + t, found)
        return found

    def reduce(sent, which, own, sib, local, sbuf, rbuf, result):
        half = chips // 2

        def contribution(offset, part):
            return jnp.concatenate([tile(offset, part, head) for head in range(HEADS_DEV)], axis=1)

        def tile(offset, part, head):
            place = lax.rem(chip + offset + chips, chips)
            block = 4 * place + 2 * core + part
            found = own[head * SLOTS + find(row, block, head)].astype(F32)
            found += sib[head * SLOTS + find(sibling, block, head)].astype(F32)
            rim = None
            if (offset, part) == (0, 0):
                rim = jnp.where(core == 1, RIM_RIGHT, ZERO)
            if (offset, part) == (0, 1):
                rim = jnp.where(core == 0, RIM_LEFT, ZERO)
            if (offset, part) == (1, 0):
                rim = jnp.where(core == 0, RIM_RIGHT, ZERO)
            if (offset, part) == (-1, 1):
                rim = jnp.where(core == 1, RIM_LEFT, ZERO)
            if rim is not None:
                found += sib[head * SLOTS + rim].astype(F32)
            return found

        edges = tree(half, True)

        def copy(way, start, end, part):
            return remote(
                sbuf.at[way, end - 1, part],
                rbuf.at[way, end - 1, part],
                sum_send.at[which, way, end - 1, part],
                sum_recv.at[which, way, end - 1, part],
                chip_at(start - end if way else end - start),
            )

        def arrived(way, distance, part):
            for start, end in edges:
                if start == distance and (end < half or way == part):
                    copy(way, start, end, part).wait_recv()
                    yield rbuf[way, end - 1, part].astype(F32)

        exchange = remote(own, sib, one_send.at[which], one_recv.at[which], to_sibling)
        exchange.start()
        exchange.wait_recv()
        sent.append(exchange)
        for start, end in sorted(edges, key=lambda edge: (-edge[0], edge[1] % 2 == 0, -edge[1])):
            for part in range(2):
                for way in range(2):
                    if end == half and part != way:
                        continue
                    total = contribution(-end if way else end, part)
                    for term in arrived(way, end, part):
                        total += term
                    sbuf[way, end - 1, part] = total.astype(BF16)
                    made = copy(way, start, end, part)
                    made.start()
                    sent.append(made)
                yield
        for part in range(2):
            total = local[part] + contribution(0, part)
            for way in range(2):
                for term in arrived(way, 0, part):
                    total += term
            result(part, total.astype(BF16))
        yield

    def keep_value_grad(part, total):
        grad_all[col, pl.ds(part * BLOCK, BLOCK)] = total

    def keep_key_grad(part, total):
        key_out[pl.ds(part * BLOCK, BLOCK)] = total

    def col_entry(place, item):
        own = 2 * place + xpos
        return own if item == 0 else 2 * place + 1 - xpos

    def project(place):
        total = acc[...]
        for part in range(2):
            total += lax.dot_general(
                grad_all[place, :, lanes(part)],
                weight_all[pl.ds(4 * place + 2 * part, 2)].reshape(2 * HEAD_DIM, HEAD_DIM),
                (((1,), (1,)), ((), ())),
                preferred_element_type=F32,
            )
        acc[...] = total

    def col_gather(sent, arrive):
        def exchange():
            return remote(
                grad_all.at[col], grad_all.at[col], one_send.at[2], one_recv.at[2], to_partner
            )

        made = exchange()
        made.start()
        sent.append(made)

        def on_arrive(offset, item):
            if arrive:
                project(col_entry(lax.rem(ypos + offset + ycount, ycount), item))

        yield from gather(
            sent,
            grad_all,
            ypos,
            ycount,
            col_entry,
            place_at,
            False,
            col_send,
            col_recv,
            second=lambda: exchange().wait_recv(),
            arrive=on_arrive,
        )

    def upstream_copy():
        return remote(input_out, up, one_send.at[3], one_recv.at[3], to_pipe)

    def key_reduce(sent):
        yield from reduce(sent, 1, k_own, k_sib, k_local, k_send, k_recv, keep_key_grad)

    def value_reduce(sent):
        yield from reduce(sent, 0, v_own, v_sib, v_local, v_send, v_recv, keep_value_grad)

    @pl.when(pipe == 1)
    def _():
        sent = []
        own_grad.start()
        drive(row_gather(sent, 0, key_all))
        for load in loads:
            load.wait()
        own_grad.wait()
        make_probs()
        value_terms()
        weights = row_gather(sent, 1, weight_all)
        drive(value_reduce(sent), take(weights, 10, 4))
        acc[...] = up[...].astype(F32)
        drive(col_gather(sent, False), weights)

        def step(place, carry):
            project(place)
            return carry

        lax.fori_loop(0, cols, step, 0)
        input_out[...] = acc[...].astype(BF16)
        made = upstream_copy()
        made.start()
        drive(row_gather(sent, 2, value_all))
        drive(key_terms())
        drive(key_reduce(sent))
        made.wait_send()
        for made in sent:
            made.wait_send()

    @pl.when(pipe == 0)
    def _():
        sent = []
        drive(row_gather(sent, 0, key_all))
        for load in loads:
            load.wait()
        make_probs()
        drive(row_gather(sent, 1, weight_all), row_gather(sent, 2, value_all))
        upstream_copy().wait_recv()
        value_terms()
        drive(value_reduce(sent), key_terms())
        acc[...] = up[...].astype(F32)
        drive(col_gather(sent, True), key_reduce(sent))
        input_out[...] = acc[...].astype(BF16)
        for made in sent:
            made.wait_send()


def body(grad_output, queries, keys, values, value_weight, random_table):
    rows = lax.axis_size("row")
    cols = lax.axis_size("col")
    tokens, features = grad_output.shape
    chips, ycount = rows // 2, cols // 2
    vmem = pl.BlockSpec(memory_space=pltpu.VMEM)
    dma = pltpu.SemaphoreType.DMA
    out = jax.ShapeDtypeStruct((tokens, features), BF16)
    ring = (2, chips // 2, 2, BLOCK, features)
    terms = (HEADS_DEV * SLOTS, BLOCK, HEAD_DIM)
    reducing = [
        pltpu.VMEM(terms, BF16),
        pltpu.VMEM(terms, BF16),
        pltpu.VMEM((2, BLOCK, features), F32),
        pltpu.VMEM(ring, BF16),
        pltpu.VMEM(ring, BF16),
    ]

    def run(*refs):
        kernel(rows, cols, *refs)

    flops = 10 * 2 * tokens * features * TILES * BLOCK + 2 * tokens * features * cols * features
    grads = pl.pallas_call(
        run,
        out_shape=(out, out, out),
        in_specs=[pl.BlockSpec(memory_space=pltpu.SMEM)] + [pl.BlockSpec(memory_space=pl.ANY)] * 5,
        out_specs=(vmem, vmem, vmem),
        scratch_shapes=[
            pltpu.VMEM((2 * rows, BLOCK, features), BF16),
            pltpu.VMEM((2 * rows, BLOCK, features), BF16),
            pltpu.VMEM((2 * rows, HEAD_DIM, HEAD_DIM), BF16),
            pltpu.VMEM((cols, tokens, features), BF16),
            pltpu.VMEM((tokens, features), BF16),
            pltpu.VMEM((tokens, features), BF16),
            pltpu.VMEM((QBLOCKS, HEADS_DEV, BLOCK, TILES * BLOCK), F32),
            pltpu.VMEM((tokens, features), F32),
            *reducing,
            *reducing,
            dma((3, 2, chips // 2, 2)),
            dma((3, 2, chips // 2, 2)),
            dma((3, chips)),
            dma((3, chips)),
            dma((2, ycount // 2, 2)),
            dma((2, ycount // 2, 2)),
            dma((2, 2, chips // 2, 2)),
            dma((2, 2, chips // 2, 2)),
            dma((4,)),
            dma((4,)),
            dma((8,)),
        ],
        compiler_params=pltpu.CompilerParams(
            collective_id=0, has_side_effects=True, vmem_limit_bytes=56 * 2**20
        ),
        cost_estimate=pl.CostEstimate(
            flops=flops, bytes_accessed=16 * tokens * features, transcendentals=0
        ),
        name="relay",
    )(
        random_table.reshape(-1),
        grad_output,
        queries[0],
        keys.reshape(2, BLOCK, features),
        values.reshape(2, BLOCK, features),
        value_weight.reshape(2, HEAD_DIM, HEAD_DIM),
    )
    return tuple(array[None] for array in grads)


def solution(mesh):
    in_specs = (
        P("row", "col"),
        P("pipe", "row", "col"),
        P("pipe", "row", "col"),
        P("pipe", "row", "col"),
        P("pipe", "col", "row"),
        P("pipe", None, "col", None),
    )
    out_specs = (P("pipe", "row", "col"), P("pipe", "row", "col"), P("pipe", "row", "col"))
    return jax.shard_map(body, mesh=mesh, in_specs=in_specs, out_specs=out_specs, check_vma=False)
```

```python
import math

import jax
import jax.numpy as jnp
from jax import lax
from jax.experimental import pallas as pl
from jax.experimental.pallas import tpu as pltpu
from jax.sharding import PartitionSpec as P

HEAD_DIM = 128
BLOCK = 64
RANDOMS = 3
QBLOCKS = 2
TILES = 3 + RANDOMS
ENTRIES = QBLOCKS * RANDOMS
ZERO, RIM_LEFT, RIM_RIGHT, SLOTS = ENTRIES, ENTRIES + 1, ENTRIES + 2, ENTRIES + 3
MESH = pl.DeviceIdType.MESH
BF16 = jnp.bfloat16
F32 = jnp.float32


def drive(*streams):
    streams = list(streams)
    while streams:
        for stream in list(streams):
            if next(stream, "end") == "end":
                streams.remove(stream)


def take(stream, delay, count):
    for _ in range(delay):
        yield
    for _ in range(count):
        if next(stream, "end") == "end":
            return
        yield


def tree(half, skip):
    if not skip:
        return [(i, i + 1) for i in range(half)]
    edges = []
    for i in range(0, half, 2):
        edges += [(i, j) for j in (i + 2, i + 1) if j <= half]
    return edges


def chain(*streams):
    for stream in streams:
        yield from stream


def lanes(head):
    return pl.ds(pl.multiple_of(head * HEAD_DIM, HEAD_DIM), HEAD_DIM)


def kernel(
    rows,
    cols,
    table_hbm,
    grad_hbm,
    query_hbm,
    key_hbm,
    value_hbm,
    weight_hbm,
    input_out,
    query_out,
    key_out,
    table_own,
    table_other,
    key_zero,
    key_one,
    value_zero,
    value_one,
    weight_all,
    grad_all,
    query,
    up,
    probs,
    acc,
    own_zero,
    own_one,
    own_two,
    own_three,
    sib_zero,
    sib_one,
    sib_two,
    sib_three,
    terms_local,
    sum_out,
    sum_in,
    part_out,
    part_in,
    last_in,
    results,
    stage,
    ring_send,
    ring_recv,
    sib_send,
    sib_recv,
    weight_send,
    weight_recv,
    share_send,
    share_recv,
    col_send,
    col_recv,
    sum_send,
    sum_recv,
    swap_send,
    swap_recv,
    part_send,
    part_recv,
    load_sem,
):
    chips = rows // 2
    ycount = cols // 2
    scale = 1.0 / math.sqrt(HEAD_DIM)
    key_all, value_all = (key_zero, key_one), (value_zero, value_one)
    terms_own = (own_zero, own_one, own_two, own_three)
    terms_sib = (sib_zero, sib_one, sib_two, sib_three)
    pipe = lax.axis_index("pipe")
    row = lax.axis_index("row")
    col = lax.axis_index("col")
    chip, core = row // 2, lax.rem(row, 2)
    ypos, xpos = col // 2, lax.rem(col, 2)
    sibling = row + 1 - 2 * core
    other_col = col + 1 - 2 * xpos
    to_sibling = {"row": sibling}
    to_pipe = {"pipe": 1 - pipe}
    quad = [(pipe, xpos), (1 - pipe, xpos), (pipe, 1 - xpos), (1 - pipe, 1 - xpos)]
    to_quad = [{"pipe": p, "col": 2 * ypos + x} for p, x in quad]

    def chip_at(hops):
        return {"row": lax.rem(row + 2 * hops + rows, rows)}

    def place_at(hops):
        return {"col": lax.rem(col + 2 * hops + cols, cols)}

    def remote(src, dst, send, recv, device):
        return pltpu.make_async_remote_copy(
            src_ref=src,
            dst_ref=dst,
            send_sem=send,
            recv_sem=recv,
            device_id=device,
            device_id_type=MESH,
        )

    def load(src, dst, slot):
        return pltpu.make_async_copy(src, dst, load_sem.at[slot])

    mine, other = lanes(pipe), lanes(1 - pipe)
    loads = [load(query_hbm.at[:, mine], query.at[pipe], 2)]
    loads.append(load(grad_hbm.at[:, mine], up.at[1], 3))
    loads.append(load(table_hbm, table_own, 4))

    def own_load(kind, section, i):
        src, dst = ((key_hbm, key_all), (value_hbm, value_all))[kind]
        slot = (0, 5)[kind] + i
        return load(src.at[i, :, mine], dst[section].at[2 * row + i], slot)

    def swap(kind, section, i):
        src, dst = ((key_hbm, key_all), (value_hbm, value_all))[kind]
        slot = (0, 4)[kind] + i
        return remote(
            src.at[i, :, other],
            dst[section].at[2 * row + i],
            swap_send.at[slot],
            swap_recv.at[slot],
            to_pipe,
        )

    def here_or_there(here, there):
        for section in range(2):
            if here is not None:
                pl.when(pipe == section)(lambda section=section: here(section))
            if there is not None:
                pl.when(pipe != section)(lambda section=section: there(section))

    def start_loads(section):
        for kind in range(2):
            for i in range(2):
                own_load(kind, section, i).start()

    def start_swaps(kind):
        def start(section):
            for i in range(2):
                swap(kind, section, i).start()

        here_or_there(start, None)

    def settle(kind):
        def here(section):
            for i in range(2):
                own_load(kind, section, i).wait()

        def there(section):
            for i in range(2):
                swap(kind, section, i).wait_recv()

        here_or_there(here, there)

    here_or_there(start_loads, None)
    for made in loads:
        made.start()

    barrier = pltpu.get_barrier_semaphore()
    greeted = [chip_at(hops) for hops in (1, -1, 2, -2)]
    greeted += [place_at(hops) for hops in ((1, -1, 2, -2) if ycount > 2 else (1, -1))]
    greeted += to_quad[1:]
    greeted += [{**device, "row": sibling} for device in to_quad]
    for device in greeted:
        pl.semaphore_signal(barrier, inc=1, device_id=device, device_id_type=MESH)
    pl.semaphore_wait(barrier, len(greeted))

    swaps = [
        remote(
            query_hbm.at[:, other], query.at[pipe], swap_send.at[2], swap_recv.at[2], to_pipe
        ),
        remote(table_hbm, table_other, swap_send.at[3], swap_recv.at[3], to_pipe),
    ]
    start_swaps(0)
    for made in swaps:
        made.start()
    start_swaps(1)
    sent = list(swaps)

    keep = (pipe == core) & (xpos == lax.rem(chip, 2))

    def weight_block():
        return weight_all.at[pipe, chip // 2, pl.ds(2 * xpos, 2)]

    def weight_move():
        return remote(
            weight_hbm,
            weight_block(),
            swap_send.at[6],
            weight_recv.at[0, chips // 2, xpos],
            {"pipe": core, "row": 2 * chip + pipe, "col": 2 * ypos + lax.rem(chip, 2)},
        )

    @pl.when(keep)
    def _():
        pltpu.make_async_copy(
            weight_hbm, weight_block(), weight_recv.at[0, chips // 2, xpos]
        ).start()

    @pl.when(jnp.logical_not(keep))
    def _():
        weight_move().start()

    def gather(buf, pos, size, entry, device_at, skip, send, recv, shared=None, arrive=None):
        half = size // 2
        edges = tree(half, skip)

        def ref(offset, item):
            return buf.at[entry(lax.rem(pos + offset + size, size), item)]

        def copy(way, start, end, item, offset):
            block = ref(offset, item)
            return remote(
                block,
                block,
                send.at[way, end - 1, item],
                recv.at[way, end - 1, item],
                device_at(start - end if way else end - start),
            )

        def push(way, distance, item):
            for start, end in edges:
                if start == distance and (end < half or way == item):
                    made = copy(way, start, end, item, distance if way else -distance)
                    made.start()
                    sent.append(made)

        for item in range(2):
            for way in range(2):
                push(way, 0, item)
        if shared is not None:
            shared(0)
        if arrive is not None:
            arrive(0, 0)
            arrive(0, 1)
        yield
        for start, end in edges:
            for item in range(2):
                ways = [way for way in range(2) if end < half or way == item]
                for way in ways:
                    copy(way, start, end, item, end if way else -end).wait_recv()
                    push(way, end, item)
                if shared is not None and item == 1:
                    for offset in (-end, end)[: 2 if end < half else 1]:
                        shared(offset)
                if arrive is not None:
                    for way in ways:
                        arrive(end if way else -end, item)
                yield

    def row_gather(which, buf, skip=True):
        shares = []

        def entry(place, item):
            return 4 * place + 2 * core + item

        def shared(offset):
            place = lax.rem(chip + offset + chips, chips)
            block = buf.at[pl.ds(4 * place + 2 * core, 2)]
            slot = (offset + chips) % chips
            made = remote(
                block, block, sib_send.at[which, slot], sib_recv.at[which, slot], to_sibling
            )
            made.start()
            shares.append(made)

        yield from gather(
            buf,
            chip,
            chips,
            entry,
            chip_at,
            skip,
            ring_send.at[which],
            ring_recv.at[which],
            shared=shared,
        )
        for made in shares:
            made.wait_recv()
        sent.extend(shares)

    def weight_gather():
        half = chips // 2
        edges = tree(half, True)
        holds = lax.rem(chip, 2) == xpos

        def place(offset):
            return lax.rem(chip + offset + chips, chips) // 2

        def copy(way, start, end, item, offset):
            block = weight_all.at[core, place(offset), pl.ds(2 * item, 2)]
            return remote(
                block,
                block,
                weight_send.at[way, end - 1, item],
                weight_recv.at[way, end - 1, item],
                chip_at(start - end if way else end - start),
            )

        def pushes(way, distance, item):
            for start, end in edges:
                if start == distance and (end < half or way == item):
                    yield copy(way, start, end, item, distance if way else -distance)

        def share(spot):
            block = weight_all.at[core, spot]
            return remote(
                block, block, share_send.at[spot], share_recv.at[spot], to_sibling
            )

        def opening():
            for item in range(2):
                block = weight_all.at[core, chip // 2, pl.ds(2 * item, 2)]
                pltpu.make_async_copy(block, block, weight_recv.at[0, half, item]).wait()
            for item in range(2):
                for way in range(2):
                    for made in pushes(way, 0, item):
                        made.start()
            share(chip // 2).start()

        pl.when(holds)(opening)
        yield
        for start, end in edges:
            for item in range(2):

                def step(start=start, end=end, item=item):
                    for way in range(2):
                        if end == half and way != item:
                            continue
                        copy(way, start, end, item, end if way else -end).wait_recv()
                        for made in pushes(way, end, item):
                            made.start()
                    if item == 1:
                        for offset in (-end, end)[: 2 if end < half else 1]:
                            share(place(offset)).start()

                pl.when(holds if end % 2 == 0 else jnp.logical_not(holds))(step)
                yield

        for spot in range(half):
            share(spot).wait_recv()

        def ending():
            for distance in range(0, half, 2):
                for item in range(2):
                    for way in range(2):
                        for made in pushes(way, distance, item):
                            made.wait_send()

        def finish():
            pl.when(holds)(ending)
            for spot in range(half):
                share(spot).wait_send()

        finishing.append(finish)

    finishing = []

    def named(section, owner):
        found = []
        for n in range(QBLOCKS):
            for t in range(RANDOMS):
                at = owner * 12 + n * 6 + pipe * 3 + t
                found.append(jnp.where(pipe == section, table_own[at], table_other[at]))
        return found

    def tiles(buf, section, n):
        block = 2 * row + n
        ids = [
            lax.rem(block + 2 * rows - 1, 2 * rows),
            block,
            lax.rem(block + 1, 2 * rows),
            *named(section, row)[n * RANDOMS : (n + 1) * RANDOMS],
        ]
        return jnp.concatenate([buf[section][i] for i in ids], axis=0)

    def rows_of(ref, section, n):
        return ref[section, pl.ds(n * BLOCK, BLOCK)]

    def make_probs(section):
        for n in range(QBLOCKS):
            scores = scale * lax.dot_general(
                rows_of(query, section, n),
                tiles(key_all, section, n),
                (((1,), (1,)), ((), ())),
                preferred_element_type=F32,
            )
            place = lax.broadcasted_iota(jnp.int32, scores.shape, 1) // BLOCK
            block = 2 * row + n
            gone_left = jnp.where(block == 0, 0, -1)
            gone_right = jnp.where(block == 2 * rows - 1, 2, -1)
            scores = jnp.where((place == gone_left) | (place == gone_right), -1e30, scores)
            top = jnp.max(scores, axis=1, keepdims=True)
            total = jnp.sum(jnp.exp(scores - top), axis=1, keepdims=True)
            probs[section, n] = jnp.exp(scores - (top + jnp.log(total)))

    def keep_terms(which, n, terms):
        terms = terms.astype(BF16)
        part = [terms[t * BLOCK : (t + 1) * BLOCK] for t in range(TILES)]
        for t in range(RANDOMS):
            terms_own[which][n * RANDOMS + t] = part[3 + t]
        if n == 0:
            terms_own[which][ZERO] = jnp.zeros_like(part[0])
            terms_own[which][RIM_LEFT] = part[0]
            terms_local[which, 0] = part[1].astype(F32)
            terms_local[which, 1] = part[2].astype(F32)
        else:
            terms_local[which, 0] += part[0].astype(F32)
            terms_local[which, 1] += part[1].astype(F32)
            terms_own[which][RIM_RIGHT] = part[2]

    def transposed_dot(left, right):
        return lax.dot_general(left, right, (((0,), (0,)), ((), ())), preferred_element_type=F32)

    def value_terms(section):
        for n in range(QBLOCKS):
            low = probs[section, n].astype(BF16)
            keep_terms(section, n, transposed_dot(low, rows_of(up, section, n)))

    def key_terms(section):
        for n in range(QBLOCKS):
            prob = probs[section, n]
            dprobs = lax.dot_general(
                rows_of(up, section, n),
                tiles(value_all, section, n),
                (((1,), (1,)), ((), ())),
                preferred_element_type=F32,
            )
            low = prob.astype(BF16).astype(F32)
            delta = jnp.sum(low * dprobs, axis=1, keepdims=True)
            dscores = (prob * (dprobs - delta) * scale).astype(BF16)
            results[section, 1, pl.ds(n * BLOCK, BLOCK)] = jnp.dot(
                dscores, tiles(key_all, section, n), preferred_element_type=F32
            ).astype(BF16)
            keep_terms(2 + section, n, transposed_dot(dscores, rows_of(query, section, n)))
            yield
        deliver(section, 1)
        yield

    outs = (input_out, query_out, key_out)

    def delivery(section, kind):
        return remote(
            results.at[section, kind],
            stage.at[kind],
            swap_send.at[7 + kind],
            swap_recv.at[7 + kind],
            to_pipe,
        )

    def deliver(section, kind):
        @pl.when(pipe == section)
        def _():
            outs[kind][:, mine] = results[section, kind]

        @pl.when(pipe != section)
        def _():
            delivery(section, kind).start()

    def reduce(section, which, result):
        half = chips // 2
        edges = tree(half, True)
        own_names, sib_names = named(section, row), named(section, sibling)

        def find(names, block):
            found = ZERO
            for slot, name in enumerate(names):
                found = jnp.where(name == block, slot, found)
            return found

        def contribution(offset, part):
            place = lax.rem(chip + offset + chips, chips)
            block = 4 * place + 2 * core + part
            total = terms_own[which][find(own_names, block)].astype(F32)
            total += terms_sib[which][find(sib_names, block)].astype(F32)
            rim = None
            if (offset, part) == (0, 0):
                rim = jnp.where(core == 1, RIM_RIGHT, ZERO)
            if (offset, part) == (0, 1):
                rim = jnp.where(core == 0, RIM_LEFT, ZERO)
            if (offset, part) == (1, 0):
                rim = jnp.where(core == 0, RIM_RIGHT, ZERO)
            if (offset, part) == (-1, 1):
                rim = jnp.where(core == 1, RIM_LEFT, ZERO)
            if rim is not None:
                total += terms_sib[which][rim].astype(F32)
            return total

        def copy(way, start, end, part):
            return remote(
                sum_out.at[which, way, end - 1, part],
                sum_in.at[which, way, end - 1, part],
                sum_send.at[which, way, end - 1, part],
                sum_recv.at[which, way, end - 1, part],
                chip_at(start - end if way else end - start),
            )

        def arrived(way, distance, part):
            for start, end in edges:
                if start == distance and (end < half or way == part):
                    copy(way, start, end, part).wait_recv()
                    yield sum_in[which, way, end - 1, part].astype(F32)

        exchange = remote(
            terms_own[which],
            terms_sib[which],
            swap_send.at[10 + which],
            swap_recv.at[10 + which],
            to_sibling,
        )
        exchange.start()
        exchange.wait_recv()
        sent.append(exchange)
        order = sorted(edges, key=lambda edge: (-edge[0], edge[1] % 2 == 0, -edge[1]))
        for start, end in order:
            for part in range(2):
                for way in range(2):
                    if end == half and part != way:
                        continue
                    total = contribution(-end if way else end, part)
                    for term in arrived(way, end, part):
                        total += term
                    sum_out[which, way, end - 1, part] = total.astype(BF16)
                    made = copy(way, start, end, part)
                    made.start()
                    sent.append(made)
                yield
        for part in range(2):
            total = terms_local[which, part] + contribution(0, part)
            for way in range(2):
                for term in arrived(way, 0, part):
                    total += term
            result(part, total.astype(BF16))
        yield

    def value_reduce(section):
        def keep_part(part, total):
            grad_all[section, 2 * ypos + part] = total

        yield from reduce(section, section, keep_part)

    def key_reduce(section):
        def keep_part(part, total):
            results[section, 2, pl.ds(part * BLOCK, BLOCK)] = total

        yield from reduce(section, 2 + section, keep_part)
        deliver(section, 2)

    def col_gather(section):
        acc[...] = jnp.zeros_like(acc)

        def arrive(offset, item):
            place = lax.rem(ypos + offset + ycount, ycount)
            acc[pl.ds(item * BLOCK, BLOCK)] += lax.dot_general(
                grad_all[section, 2 * place + item],
                weight_all[section, place].reshape(4 * HEAD_DIM, HEAD_DIM),
                (((1,), (1,)), ((), ())),
                preferred_element_type=F32,
            )

        yield from gather(
            grad_all.at[section],
            ypos,
            ycount,
            lambda place, item: 2 * place + item,
            place_at,
            True,
            col_send.at[section],
            col_recv.at[section],
            arrive=arrive,
        )

    def own_share():
        return acc[:, lanes(2 * xpos + pipe)]

    def spread_partials():
        for head in range(4):
            part_out[1, head] = acc[:, lanes(head)].astype(BF16)
        copies = [
            remote(
                part_out.at[1, 2 * x + p],
                part_in.at[j],
                part_send.at[1, j],
                part_recv.at[1, j],
                to_quad[j],
            )
            for j, (p, x) in enumerate(quad)
            if j
        ]
        for made in copies:
            made.start()
        sent.extend(copies)
        return copies

    def last_copy(j):
        x = quad[j][1]
        return remote(
            part_out.at[0, pl.ds(2 * x, 2)],
            last_in.at[j],
            part_send.at[0, j],
            part_recv.at[0, j],
            {"pipe": 0, "col": 2 * ypos + x},
        )

    def last_projection():
        yield from col_gather(0)
        acc[:, lanes(2 * xpos + pipe)] += up[0].astype(F32)
        for head in range(4):
            part_out[0, head] = acc[:, lanes(head)].astype(BF16)

        @pl.when(pipe == 1)
        def _():
            for j in (1, 3):
                last_copy(j).start()

        @pl.when(pipe == 0)
        def _():
            last_copy(2).start()

        yield

    settle(0)
    weights = weight_gather()
    drive(row_gather(0, key_all[1]), take(weights, 4, 8))
    for made in loads:
        made.wait()
    for made in swaps:
        made.wait_recv()
    make_probs(1)
    value_terms(1)
    drive(value_reduce(1), weights)
    settle(1)
    drive(col_gather(1), row_gather(1, key_all[0]), row_gather(2, value_all[1]))
    partials = spread_partials()
    make_probs(0)
    total = up[1].astype(F32) + own_share()
    for j, made in enumerate(partials, 1):
        made.wait_recv()
        total += part_in[j].astype(F32)
    results[1, 0] = total.astype(BF16)
    up[0] = results[1, 0]
    value_terms(0)
    deliver(1, 0)
    drive(value_reduce(0), chain(row_gather(3, value_all[0]), key_terms(1)))
    drive(last_projection(), key_reduce(1), chain(key_terms(0), key_reduce(0)))

    @pl.when(pipe == 0)
    def _():
        delivery(1, 0).wait_send()
        for j in (1, 2, 3):
            last_copy(j).wait_recv()
        for head in range(2):
            total = acc[:, lanes(2 * xpos + head)]
            for j in (1, 2, 3):
                total += last_in[j, head].astype(F32)
            input_out[:, lanes(head)] = total.astype(BF16)
        last_copy(2).wait_send()

    @pl.when(pipe == 1)
    def _():
        delivery(1, 0).wait_recv()
        input_out[:, other] = stage[0]
        for j in (1, 3):
            last_copy(j).wait_send()

    for kind in (1, 2):
        delivery(1, kind).wait_recv()
        outs[kind][:, other] = stage[kind]
        here_or_there(None, lambda section, kind=kind: delivery(section, kind).wait_send())

    @pl.when(jnp.logical_not(keep))
    def _():
        weight_move().wait_send()

    def swaps_left(section):
        for kind in range(2):
            for i in range(2):
                swap(kind, section, i).wait_send()

    here_or_there(swaps_left, None)
    for finish in finishing:
        finish()
    for made in sent:
        made.wait_send()


def body(grad_output, queries, keys, values, value_weight, random_table):
    rows = lax.axis_size("row")
    cols = lax.axis_size("col")
    tokens, features = grad_output.shape
    half = rows // 4
    ycount = cols // 2
    vmem = pl.BlockSpec(memory_space=pltpu.VMEM)
    hbm = pl.BlockSpec(memory_space=pl.ANY)
    dma = pltpu.SemaphoreType.DMA
    out = jax.ShapeDtypeStruct((tokens, features), BF16)
    tile = (BLOCK, HEAD_DIM)
    block = (tokens, HEAD_DIM)

    def run(*refs):
        kernel(rows, cols, *refs)

    flops = 10 * 2 * tokens * features * TILES * BLOCK + 2 * tokens * features * cols * features
    grads = pl.pallas_call(
        run,
        out_shape=(out, out, out),
        in_specs=[hbm] * 6,
        out_specs=(vmem, vmem, vmem),
        scratch_shapes=[
            pltpu.SMEM((random_table.size,), jnp.int32),
            pltpu.SMEM((random_table.size,), jnp.int32),
            *[pltpu.VMEM((2 * rows, *tile), BF16)] * 4,
            pltpu.VMEM((2, ycount, 4, HEAD_DIM, HEAD_DIM), BF16),
            pltpu.VMEM((2, 2 * ycount, *tile), BF16),
            pltpu.VMEM((2, *block), BF16),
            pltpu.VMEM((2, *block), BF16),
            pltpu.VMEM((2, QBLOCKS, BLOCK, TILES * BLOCK), F32),
            pltpu.VMEM((tokens, 4 * HEAD_DIM), F32),
            *[pltpu.VMEM((SLOTS, *tile), BF16)] * 8,
            pltpu.VMEM((4, 2, *tile), F32),
            pltpu.VMEM((4, 2, half, 2, *tile), BF16),
            pltpu.VMEM((4, 2, half, 2, *tile), BF16),
            pltpu.VMEM((2, 4, *block), BF16),
            pltpu.VMEM((4, *block), BF16),
            pltpu.VMEM((4, 2, *block), BF16),
            pltpu.VMEM((2, 3, *block), BF16),
            pltpu.VMEM((3, *block), BF16),
            dma((4, 2, half, 2)),
            dma((4, 2, half, 2)),
            dma((4, 2 * half)),
            dma((4, 2 * half)),
            dma((2, half, 2)),
            dma((2, half + 1, 2)),
            dma((half,)),
            dma((half,)),
            dma((2, 2, ycount // 2, 2)),
            dma((2, 2, ycount // 2, 2)),
            dma((4, 2, half, 2)),
            dma((4, 2, half, 2)),
            dma((14,)),
            dma((14,)),
            dma((2, 4)),
            dma((2, 4)),
            dma((7,)),
        ],
        compiler_params=pltpu.CompilerParams(
            collective_id=0, has_side_effects=True, vmem_limit_bytes=56 * 2**20
        ),
        cost_estimate=pl.CostEstimate(
            flops=flops, bytes_accessed=16 * tokens * features, transcendentals=0
        ),
        name="relay",
    )(
        random_table.reshape(-1),
        grad_output,
        queries[0],
        keys.reshape(2, BLOCK, features),
        values.reshape(2, BLOCK, features),
        value_weight.reshape(2, HEAD_DIM, HEAD_DIM),
    )
    return tuple(array[None] for array in grads)


def solution(mesh):
    in_specs = (
        P("row", "col"),
        P("pipe", "row", "col"),
        P("pipe", "row", "col"),
        P("pipe", "row", "col"),
        P("pipe", "col", "row"),
        P("pipe", None, "col", None),
    )
    out_specs = (P("pipe", "row", "col"), P("pipe", "row", "col"), P("pipe", "row", "col"))
    return jax.shard_map(body, mesh=mesh, in_specs=in_specs, out_specs=out_specs, check_vma=False)
```

```python
import math

import jax
import jax.numpy as jnp
from jax import lax
from jax.experimental import pallas as pl
from jax.experimental.pallas import tpu as pltpu
from jax.sharding import PartitionSpec as P

HEAD_DIM = 128
BLOCK = 64
RANDOMS = 3
HEADS_DEV = 2
QBLOCKS = 2
TILES = 3 + RANDOMS
ENTRIES = QBLOCKS * RANDOMS
ZERO, RIM_LEFT, RIM_RIGHT, SLOTS = ENTRIES, ENTRIES + 1, ENTRIES + 2, ENTRIES + 3
MESH = pl.DeviceIdType.MESH
BF16 = jnp.bfloat16
F32 = jnp.float32


def drive(*streams):
    streams = list(streams)
    while streams:
        for stream in list(streams):
            if next(stream, "end") == "end":
                streams.remove(stream)


def take(stream, delay, count):
    for _ in range(delay):
        yield
    for _ in range(count):
        if next(stream, "end") == "end":
            return
        yield


def tree(half, skip):
    if not skip:
        return [(i, i + 1) for i in range(half)]
    edges = []
    for i in range(0, half, 2):
        edges += [(i, j) for j in (i + 2, i + 1) if j <= half]
    return edges


def chain(*streams):
    for stream in streams:
        yield from stream


def lanes(head):
    return pl.ds(head * HEAD_DIM, HEAD_DIM)


def kernel(
    rows,
    cols,
    table,
    grad,
    query_hbm,
    key,
    value,
    weight,
    input_out,
    query_out,
    key_out,
    key_all,
    value_all,
    weight_all,
    grad_all,
    query,
    up,
    probs,
    acc,
    v_own,
    v_sib,
    v_local,
    v_send,
    v_recv,
    k_own,
    k_sib,
    k_local,
    k_send,
    k_recv,
    ring_send,
    ring_recv,
    sib_send,
    sib_recv,
    col_send,
    col_recv,
    sum_send,
    sum_recv,
    one_send,
    one_recv,
    load_sem,
):
    chips = rows // 2
    ycount = cols // 2
    scale = 1.0 / math.sqrt(HEAD_DIM)
    pipe = lax.axis_index("pipe")
    row = lax.axis_index("row")
    col = lax.axis_index("col")
    chip, core = row // 2, lax.rem(row, 2)
    ypos, xpos = col // 2, lax.rem(col, 2)
    sibling = row + 1 - 2 * core

    def chip_at(hops):
        return {"row": lax.rem(row + 2 * hops + rows, rows)}

    def place_at(hops):
        return {"col": lax.rem(col + 2 * hops + cols, cols)}

    to_sibling = {"row": sibling}
    to_partner = {"col": col + 1 - 2 * xpos}
    to_pipe = {"pipe": 1 - pipe}

    own_key = [
        pltpu.make_async_copy(key.at[i], key_all.at[2 * row + i], load_sem.at[i]) for i in range(2)
    ]
    loads = [
        pltpu.make_async_copy(weight.at[i], weight_all.at[2 * row + i], load_sem.at[2 + i])
        for i in range(2)
    ]
    loads += [
        pltpu.make_async_copy(value.at[i], value_all.at[2 * row + i], load_sem.at[4 + i])
        for i in range(2)
    ]
    loads.append(pltpu.make_async_copy(query_hbm, query, load_sem.at[6]))
    own_grad = pltpu.make_async_copy(grad, up, load_sem.at[7])
    for load in own_key + loads:
        load.start()

    barrier = pltpu.get_barrier_semaphore()
    greeted = [chip_at(hops) for hops in (1, -1, 2, -2)]
    greeted += [place_at(1), place_at(-1), to_sibling, to_partner, to_pipe]
    for device in greeted:
        pl.semaphore_signal(barrier, inc=1, device_id=device, device_id_type=MESH)
    for load in own_key:
        load.wait()
    pl.semaphore_wait(barrier, len(greeted))

    def remote(src, dst, send, recv, device):
        return pltpu.make_async_remote_copy(
            src_ref=src,
            dst_ref=dst,
            send_sem=send,
            recv_sem=recv,
            device_id=device,
            device_id_type=MESH,
        )

    def gather(sent, buf, pos, size, entry, device_at, skip, send, recv, shared=None, second=None, arrive=None, joined=False):
        half = size // 2
        edges = tree(half, skip)

        def ref(offset, item):
            return buf.at[entry(lax.rem(pos + offset + size, size), item)]

        def copy(way, start, end, item, offset):
            block = ref(offset, item)
            if joined and end < half:
                place = lax.rem(pos + offset + size, size)
                block = buf.at[pl.ds(entry(place, 0), 2)]
            return remote(
                block,
                block,
                send.at[way, end - 1, item],
                recv.at[way, end - 1, item],
                device_at(start - end if way else end - start),
            )

        def push_all(distance):
            for start, end in edges:
                if start == distance:
                    for way in range(2):
                        made = copy(way, start, end, way, distance if way else -distance)
                        made.start()
                        sent.append(made)

        def push(way, distance, item):
            for start, end in edges:
                if start == distance and (end < half or way == item):
                    made = copy(way, start, end, item, distance if way else -distance)
                    made.start()
                    sent.append(made)

        if joined:
            push_all(0)
            shared(0)
            yield
            for start, end in edges:
                for way in range(2):
                    copy(way, start, end, way, end if way else -end).wait_recv()
                push_all(end)
                for offset in (-end, end)[: 2 if end < half else 1]:
                    shared(offset)
                yield
            return

        for item in range(2):
            if item == 1 and second is not None:
                second()
            for way in range(2):
                push(way, 0, item)
        if shared is not None:
            shared(0)
        if arrive is not None:
            arrive(0, 0)
            arrive(0, 1)
        yield
        for start, end in edges:
            for item in range(2):
                ways = [way for way in range(2) if end < half or way == item]
                for way in ways:
                    copy(way, start, end, item, end if way else -end).wait_recv()
                    push(way, end, item)
                if shared is not None and item == 1:
                    for offset in (-end, end)[: 2 if end < half else 1]:
                        shared(offset)
                if arrive is not None:
                    for way in ways:
                        arrive(end if way else -end, item)
                yield

    def row_gather(sent, which, buf, skip=True):
        shares = []

        def entry(place, item):
            return 4 * place + 2 * core + item

        def shared(offset):
            place = lax.rem(chip + offset + chips, chips)
            block = buf.at[pl.ds(4 * place + 2 * core, 2)]
            slot = (offset + chips) % chips
            made = remote(
                block, block, sib_send.at[which, slot], sib_recv.at[which, slot], to_sibling
            )
            made.start()
            shares.append(made)

        yield from gather(
            sent,
            buf,
            chip,
            chips,
            entry,
            chip_at,
            skip,
            ring_send.at[which],
            ring_recv.at[which],
            shared=shared,
            joined=True,
        )
        for made in shares:
            made.wait_recv()
        sent.extend(shares)

    def tile_ids(n, head):
        block = 2 * row + n
        ids = [
            lax.rem(block + 2 * rows - 1, 2 * rows),
            block,
            lax.rem(block + 1, 2 * rows),
        ]
        for t in range(RANDOMS):
            ids.append(table[row * 12 + n * 6 + head * 3 + t])
        return ids

    def tiles(buf, n, head):
        return jnp.concatenate([buf[i, :, lanes(head)] for i in tile_ids(n, head)], axis=0)

    def rows_of(ref, n, head):
        return ref[pl.ds(n * BLOCK, BLOCK), lanes(head)]

    def make_probs():
        for n in range(QBLOCKS):
            for head in range(HEADS_DEV):
                scores = scale * lax.dot_general(
                    rows_of(query, n, head),
                    tiles(key_all, n, head),
                    (((1,), (1,)), ((), ())),
                    preferred_element_type=F32,
                )
                place = lax.broadcasted_iota(jnp.int32, scores.shape, 1) // BLOCK
                block = 2 * row + n
                gone = jnp.where(block == 0, 0, -1)
                gone_right = jnp.where(block == 2 * rows - 1, 2, -1)
                scores = jnp.where((place == gone) | (place == gone_right), -1e30, scores)
                top = jnp.max(scores, axis=1, keepdims=True)
                total = jnp.sum(jnp.exp(scores - top), axis=1, keepdims=True)
                probs[n, head] = jnp.exp(scores - (top + jnp.log(total)))

    def keep_terms(n, head, terms, own, local):
        terms = terms.astype(BF16)
        part = [terms[t * BLOCK : (t + 1) * BLOCK] for t in range(TILES)]
        for t in range(RANDOMS):
            own[head * SLOTS + n * RANDOMS + t] = part[3 + t]
        if n == 0:
            own[head * SLOTS + ZERO] = jnp.zeros_like(part[0])
            own[head * SLOTS + RIM_LEFT] = part[0]
            local[0, :, lanes(head)] = part[1].astype(F32)
            local[1, :, lanes(head)] = part[2].astype(F32)
        else:
            local[0, :, lanes(head)] += part[0].astype(F32)
            local[1, :, lanes(head)] += part[1].astype(F32)
            own[head * SLOTS + RIM_RIGHT] = part[2]

    def transposed_dot(left, right):
        return lax.dot_general(left, right, (((0,), (0,)), ((), ())), preferred_element_type=F32)

    def value_terms():
        for n in range(QBLOCKS):
            for head in range(HEADS_DEV):
                low = probs[n, head].astype(BF16)
                keep_terms(n, head, transposed_dot(low, rows_of(up, n, head)), v_own, v_local)

    def key_terms():
        for n in range(QBLOCKS):
            for head in range(HEADS_DEV):
                prob = probs[n, head]
                dprobs = lax.dot_general(
                    rows_of(up, n, head),
                    tiles(value_all, n, head),
                    (((1,), (1,)), ((), ())),
                    preferred_element_type=F32,
                )
                low = prob.astype(BF16).astype(F32)
                delta = jnp.sum(low * dprobs, axis=1, keepdims=True)
                dscores = (prob * (dprobs - delta) * scale).astype(BF16)
                query_out[pl.ds(n * BLOCK, BLOCK), lanes(head)] = jnp.dot(
                    dscores, tiles(key_all, n, head), preferred_element_type=F32
                ).astype(BF16)
                keep_terms(
                    n, head, transposed_dot(dscores, rows_of(query, n, head)), k_own, k_local
                )
                yield

    def find(owner, block, head):
        found = ZERO
        for n in range(QBLOCKS):
            for t in range(RANDOMS):
                named = table[owner * 12 + n * 6 + head * 3 + t]
                found = jnp.where(named == block, n * RANDOMS + t, found)
        return found

    def reduce(sent, which, own, sib, local, sbuf, rbuf, result):
        half = chips // 2

        def contribution(offset, part):
            return jnp.concatenate([tile(offset, part, head) for head in range(HEADS_DEV)], axis=1)

        def tile(offset, part, head):
            place = lax.rem(chip + offset + chips, chips)
            block = 4 * place + 2 * core + part
            found = own[head * SLOTS + find(row, block, head)].astype(F32)
            found += sib[head * SLOTS + find(sibling, block, head)].astype(F32)
            rim = None
            if (offset, part) == (0, 0):
                rim = jnp.where(core == 1, RIM_RIGHT, ZERO)
            if (offset, part) == (0, 1):
                rim = jnp.where(core == 0, RIM_LEFT, ZERO)
            if (offset, part) == (1, 0):
                rim = jnp.where(core == 0, RIM_RIGHT, ZERO)
            if (offset, part) == (-1, 1):
                rim = jnp.where(core == 1, RIM_LEFT, ZERO)
            if rim is not None:
                found += sib[head * SLOTS + rim].astype(F32)
            return found

        edges = tree(half, True)

        def copy(way, start, end):
            parts = pl.ds(0, 2) if end < half else pl.ds(way, 1)
            return remote(
                sbuf.at[way, end - 1, parts],
                rbuf.at[way, end - 1, parts],
                sum_send.at[which, way, end - 1, 0],
                sum_recv.at[which, way, end - 1, 0],
                chip_at(start - end if way else end - start),
            )

        def wait_for(way, distance):
            for start, end in edges:
                if start == distance:
                    copy(way, start, end).wait_recv()

        def arrived(way, distance, part):
            for start, end in edges:
                if start == distance and (end < half or way == part):
                    yield rbuf[way, end - 1, part].astype(F32)

        exchange = remote(own, sib, one_send.at[which], one_recv.at[which], to_sibling)
        exchange.start()
        exchange.wait_recv()
        sent.append(exchange)
        for start, end in sorted(edges, key=lambda edge: (-edge[0], edge[1] % 2 == 0, -edge[1])):
            for way in range(2):
                parts = range(2) if end < half else [way]
                totals = [contribution(-end if way else end, part) for part in parts]
                wait_for(way, end)
                for part, total in zip(parts, totals):
                    for term in arrived(way, end, part):
                        total += term
                    sbuf[way, end - 1, part] = total.astype(BF16)
                made = copy(way, start, end)
                made.start()
                sent.append(made)
            yield
        totals = [local[part] + contribution(0, part) for part in range(2)]
        for way in range(2):
            wait_for(way, 0)
        for part, total in enumerate(totals):
            for way in range(2):
                for term in arrived(way, 0, part):
                    total += term
            result(part, total.astype(BF16))
        yield

    def keep_value_grad(part, total):
        grad_all[col, pl.ds(part * BLOCK, BLOCK)] = total

    def keep_key_grad(part, total):
        key_out[pl.ds(part * BLOCK, BLOCK)] = total

    def col_entry(place, item):
        own = 2 * place + xpos
        return own if item == 0 else 2 * place + 1 - xpos

    def project(place):
        total = acc[...]
        for part in range(2):
            total += lax.dot_general(
                grad_all[place, :, lanes(part)],
                weight_all[pl.ds(4 * place + 2 * part, 2)].reshape(2 * HEAD_DIM, HEAD_DIM),
                (((1,), (1,)), ((), ())),
                preferred_element_type=F32,
            )
        acc[...] = total

    def col_gather(sent, arrive):
        def exchange():
            return remote(
                grad_all.at[col], grad_all.at[col], one_send.at[2], one_recv.at[2], to_partner
            )

        made = exchange()
        made.start()
        sent.append(made)

        def on_arrive(offset, item):
            if arrive:
                project(col_entry(lax.rem(ypos + offset + ycount, ycount), item))

        yield from gather(
            sent,
            grad_all,
            ypos,
            ycount,
            col_entry,
            place_at,
            False,
            col_send,
            col_recv,
            second=lambda: exchange().wait_recv(),
            arrive=on_arrive,
        )

    def upstream_copy():
        return remote(input_out, up, one_send.at[3], one_recv.at[3], to_pipe)

    def key_reduce(sent):
        yield from reduce(sent, 1, k_own, k_sib, k_local, k_send, k_recv, keep_key_grad)

    def value_reduce(sent):
        yield from reduce(sent, 0, v_own, v_sib, v_local, v_send, v_recv, keep_value_grad)

    @pl.when(pipe == 1)
    def _():
        sent = []
        own_grad.start()
        drive(row_gather(sent, 0, key_all))
        for load in loads:
            load.wait()
        own_grad.wait()
        make_probs()
        value_terms()
        weights = row_gather(sent, 1, weight_all)
        drive(value_reduce(sent), take(weights, 4, 3))
        acc[...] = up[...].astype(F32)
        drive(col_gather(sent, False), weights)

        def step(place, carry):
            project(place)
            return carry

        lax.fori_loop(0, cols, step, 0)
        input_out[...] = acc[...].astype(BF16)
        made = upstream_copy()
        made.start()
        drive(row_gather(sent, 2, value_all))
        drive(key_terms())
        drive(key_reduce(sent))
        made.wait_send()
        for made in sent:
            made.wait_send()

    @pl.when(pipe == 0)
    def _():
        sent = []
        drive(row_gather(sent, 0, key_all))
        for load in loads:
            load.wait()
        make_probs()
        drive(row_gather(sent, 1, weight_all), row_gather(sent, 2, value_all))
        upstream_copy().wait_recv()
        value_terms()
        keys = chain(key_terms(), key_reduce(sent))
        drive(value_reduce(sent), take(keys, 1, 7))
        acc[...] = up[...].astype(F32)
        drive(col_gather(sent, True), keys)
        input_out[...] = acc[...].astype(BF16)
        for made in sent:
            made.wait_send()


def body(grad_output, queries, keys, values, value_weight, random_table):
    rows = lax.axis_size("row")
    cols = lax.axis_size("col")
    tokens, features = grad_output.shape
    chips, ycount = rows // 2, cols // 2
    vmem = pl.BlockSpec(memory_space=pltpu.VMEM)
    dma = pltpu.SemaphoreType.DMA
    out = jax.ShapeDtypeStruct((tokens, features), BF16)
    ring = (2, chips // 2, 2, BLOCK, features)
    terms = (HEADS_DEV * SLOTS, BLOCK, HEAD_DIM)
    reducing = [
        pltpu.VMEM(terms, BF16),
        pltpu.VMEM(terms, BF16),
        pltpu.VMEM((2, BLOCK, features), F32),
        pltpu.VMEM(ring, BF16),
        pltpu.VMEM(ring, BF16),
    ]

    def run(*refs):
        kernel(rows, cols, *refs)

    flops = 10 * 2 * tokens * features * TILES * BLOCK + 2 * tokens * features * cols * features
    grads = pl.pallas_call(
        run,
        out_shape=(out, out, out),
        in_specs=[pl.BlockSpec(memory_space=pltpu.SMEM)] + [pl.BlockSpec(memory_space=pl.ANY)] * 5,
        out_specs=(vmem, vmem, vmem),
        scratch_shapes=[
            pltpu.VMEM((2 * rows, BLOCK, features), BF16),
            pltpu.VMEM((2 * rows, BLOCK, features), BF16),
            pltpu.VMEM((2 * rows, HEAD_DIM, HEAD_DIM), BF16),
            pltpu.VMEM((cols, tokens, features), BF16),
            pltpu.VMEM((tokens, features), BF16),
            pltpu.VMEM((tokens, features), BF16),
            pltpu.VMEM((QBLOCKS, HEADS_DEV, BLOCK, TILES * BLOCK), F32),
            pltpu.VMEM((tokens, features), F32),
            *reducing,
            *reducing,
            dma((3, 2, chips // 2, 2)),
            dma((3, 2, chips // 2, 2)),
            dma((3, chips)),
            dma((3, chips)),
            dma((2, ycount // 2, 2)),
            dma((2, ycount // 2, 2)),
            dma((2, 2, chips // 2, 2)),
            dma((2, 2, chips // 2, 2)),
            dma((4,)),
            dma((4,)),
            dma((8,)),
        ],
        compiler_params=pltpu.CompilerParams(
            collective_id=0, has_side_effects=True, vmem_limit_bytes=56 * 2**20
        ),
        cost_estimate=pl.CostEstimate(
            flops=flops, bytes_accessed=16 * tokens * features, transcendentals=0
        ),
        name="relay",
    )(
        random_table.reshape(-1),
        grad_output,
        queries[0],
        keys.reshape(2, BLOCK, features),
        values.reshape(2, BLOCK, features),
        value_weight.reshape(2, HEAD_DIM, HEAD_DIM),
    )
    return tuple(array[None] for array in grads)


def solution(mesh):
    in_specs = (
        P("row", "col"),
        P("pipe", "row", "col"),
        P("pipe", "row", "col"),
        P("pipe", "row", "col"),
        P("pipe", "col", "row"),
        P("pipe", None, "col", None),
    )
    out_specs = (P("pipe", "row", "col"), P("pipe", "row", "col"), P("pipe", "row", "col"))
    return jax.shard_map(body, mesh=mesh, in_specs=in_specs, out_specs=out_specs, check_vma=False)
```
